32 devices in a mesh: svc: 16 (over z, y, core), tm: 2 (over x).
Axes of the slice: x: 2, y: 2, z: 4, core: 2. Of those that a mesh axis runs over, the one named last changes fastest.
Arguments:
- metrics: bfloat16 [8192, 4096], P('svc', 'tm'), may hold values from -15 to 15
- band_starts: int32 [4], replicated, may hold values from 1 to 2015
Outputs:
- cross: bfloat16 [4, 2, 8192, 8192], P(None, None, 'svc', 'tm')
- coherence: float32 [4, 8192, 8192], P(None, 'svc', 'tm')
The draws below stay inside these ranges and needn't reach their ends.
Inputs may be any that keep to these rules, and one draw needn't show every extreme that they name: `band_starts`: each band covers 32 consecutive bins starting at its entry.
All inputs are finite; a program needn't handle non-finite values.
Results may differ from the reference program's by a relative error of at most 0.0066.
Values may be sent and summed in bfloat16 or wider, within the bound.
A program may use at most 192 MiB of HBM per device.

```python
import jax
import jax.numpy as jnp
from jax import lax

CHANNELS = 8192
TLEN = 4096
BANDS = 4
BINS = 32


def draw_metrics(key, part):
    key_scale, key_base = jax.random.split(key, 2)
    scales = jnp.exp(jax.random.uniform(key_scale, (CHANNELS, 1), jnp.float32, jnp.log(0.3), jnp.log(3.0)))
    values = jnp.clip(jax.random.normal(key_base, (CHANNELS, TLEN), jnp.float32), -5.0, 5.0)
    return (scales * values).astype(jnp.bfloat16)


def plant(array, own_key, low, top_value):
    shape = array.shape
    index_at = [jax.random.randint(jax.random.fold_in(own_key, axis), (), 0, shape[axis]) for axis in range(len(shape))]
    array = array.at[tuple(index_at)].set(low)
    longest = shape.index(max(shape))
    index_at[longest] = (index_at[longest] + 1) % shape[longest]
    return array.at[tuple(index_at)].set(top_value)


def setup_inputs(seed: int = 0) -> dict:
    arg_keys = jax.random.split(jax.random.key(seed), 3)
    return {
        "metrics": draw_metrics(jax.random.fold_in(arg_keys[2], 71), 0),
        "band_starts": plant(jax.random.randint(arg_keys[1], (BANDS,), 1, TLEN // 2 - BINS), jax.random.fold_in(arg_keys[1], 1), 1, (TLEN // 2 - BINS) - 1).astype(jnp.int32),
    }


epsilon = 1e-06

def make_table(minutes, band_starts):
    offsets = jnp.arange(BINS, dtype=jnp.int32)
    freqs = band_starts.astype(jnp.int32)[:, None] + offsets[None, :]
    phase_index = minutes[:, None, None] * freqs[None, :, :] % TLEN
    phases = 2.0 * jnp.pi / TLEN * phase_index.astype(jnp.float32)
    norm = 1.0 / jnp.sqrt(jnp.float32(TLEN))
    stacked = jnp.stack([jnp.cos(phases) * norm, -jnp.sin(phases) * norm], axis=2)
    return stacked.reshape(minutes.shape[0], BANDS * 2 * BINS).astype(jnp.bfloat16)

def band_products(row_spec, col_spec):
    swapped = jnp.concatenate([row_spec[:, BINS:], -row_spec[:, :BINS]], axis=1)
    dims = (((1,), (1,)), ((), ()))
    real_part = lax.dot_general(row_spec, col_spec, dims, preferred_element_type=jnp.float32) / BINS
    imag_part = lax.dot_general(swapped, col_spec, dims, preferred_element_type=jnp.float32) / BINS
    row_power = lax.optimization_barrier(jnp.sum(jnp.square(row_spec.astype(jnp.float32)), axis=1)) / BINS
    col_power = lax.optimization_barrier(jnp.sum(jnp.square(col_spec.astype(jnp.float32)), axis=1)) / BINS
    coherence = (real_part * real_part + imag_part * imag_part) / ((row_power[:, None] + epsilon) * (col_power[None, :] + epsilon))
    cross = jnp.stack([real_part, imag_part], axis=0).astype(jnp.bfloat16)
    return (cross, coherence)

def reference(metrics, band_starts):
    minutes = jnp.arange(TLEN, dtype=jnp.int32)
    dft_table = make_table(minutes, band_starts)
    spectra = jnp.dot(metrics, dft_table, preferred_element_type=jnp.float32).astype(jnp.bfloat16)
    cross_list = []
    coherence_list = []
    for band in range(BANDS):
        offset = band * 2 * BINS
        block = spectra[:, offset:offset + 2 * BINS]
        cross, coherence = band_products(block, block)
        cross_list.append(cross)
        coherence_list.append(coherence)
    return (jnp.stack(cross_list, axis=0), jnp.stack(coherence_list, axis=0))
```

```python
import functools
import math

import jax
import jax.numpy as jnp
from jax import lax
from jax.experimental import pallas as pl
from jax.experimental.pallas import tpu as pltpu
from jax.sharding import PartitionSpec as P

BANDS = 4
BINS = 32
WIDTH = BANDS * 2 * BINS
EPSILON = 1e-06
SPLIT = 64
CHUNKS = 2
LAG = 2
MESH = pl.DeviceIdType.MESH
NT = (((1,), (1,)), ((), ()))


def fill_table(table, starts, first_minute, tlen):
    minutes = table.shape[0]
    lane = lax.broadcasted_iota(jnp.int32, (1, WIDTH), 1)
    band = lane // (2 * BINS)
    start = jnp.zeros((1, WIDTH), jnp.int32)
    for b in range(BANDS):
        start = jnp.where(band == b, starts[b], start)
    freq = start + lane % BINS
    quarter = (lane // BINS) % 2 * (tlen // 4)
    unit = 2.0 * math.pi / tlen
    outer = minutes // SPLIT
    ta = first_minute + SPLIT * lax.broadcasted_iota(jnp.int32, (outer, WIDTH), 0)
    angle_a = ((ta * freq) & (tlen - 1)).astype(jnp.float32) * unit
    tb = lax.broadcasted_iota(jnp.int32, (SPLIT, WIDTH), 0)
    angle_b = ((tb * freq + quarter) & (tlen - 1)).astype(jnp.float32) * unit
    norm = 1.0 / math.sqrt(tlen)
    cos_a, sin_a = jnp.cos(angle_a), jnp.sin(angle_a)
    cos_b, sin_b = jnp.cos(angle_b) * norm, jnp.sin(angle_b) * norm
    for a in range(outer):
        rows = cos_a[a : a + 1] * cos_b - sin_a[a : a + 1] * sin_b
        table[a * SPLIT : (a + 1) * SPLIT, :] = rows.astype(jnp.bfloat16)


def spectra_kernel(
    S, T, starts, metrics_hbm, cols, lhs, rinv,
    metrics, table, partial, landed, rows,
    in_sem, rs_send, rs_recv, ag_send, ag_recv, up_send, down_send, z_recv, y_send, y_recv, c_send, c_recv,
):
    s, t = lax.axis_index("svc"), lax.axis_index("tm")
    R, L = metrics.shape
    piece = R // T
    size = piece // CHUNKS
    Z, ZP = S // 4, S // T // 4
    z, y, c = s // 4, (s // 2) % 2, s % 2
    z0 = t * ZP
    own_z = z - z0
    in_panel = (own_z >= 0) & (own_z < ZP)
    near = jnp.clip(own_z, 0, ZP - 1)
    y_mate = (z * 4 + (1 - y) * 2 + c, t)
    c_mate = (z * 4 + y * 2 + 1 - c, t)
    z_up = (lax.rem(z + 1, Z) * 4 + y * 2 + c, t)
    z_down = (lax.rem(z + Z - 1, Z) * 4 + y * 2 + c, t)

    load = pltpu.make_async_copy(metrics_hbm, metrics, in_sem)
    load.start()
    barrier = pltpu.get_barrier_semaphore()
    for i in range(1, T):
        pl.semaphore_signal(barrier, inc=1, device_id=(s, lax.rem(t + i, T)), device_id_type=MESH)
    for mate in (y_mate, c_mate, z_up, z_down):
        pl.semaphore_signal(barrier, inc=1, device_id=mate, device_id_type=MESH)

    fill_table(table, starts, t * L, T * L)
    load.wait()

    def transform(first):
        return jnp.dot(metrics[pl.ds(first, size), :], table[...], preferred_element_type=jnp.float32)

    def remote(src, dst, send, recv, to):
        return pltpu.make_async_remote_copy(
            src_ref=src, dst_ref=dst, send_sem=send, recv_sem=recv, device_id=to, device_id_type=MESH
        )

    def rs_copy(i, ch):
        part = pl.ds(ch * size, size)
        to = (s, lax.rem(t + 1 + i, T))
        return remote(partial.at[i, part], landed.at[i, part], rs_send.at[i, ch], rs_recv.at[i, ch], to)

    for i in range(T - 1):
        for ch in range(CHUNKS):
            target = lax.rem(t + 1 + i, T)
            partial[i, pl.ds(ch * size, size), :] = transform(pl.multiple_of(target * piece + ch * size, size))
            if i == 0 and ch == 0:
                pl.semaphore_wait(barrier, T - 1 + 4)
            rs_copy(i, ch).start()
    for ch in range(CHUNKS):
        partial[T - 1, pl.ds(ch * size, size), :] = transform(pl.multiple_of(t * piece + ch * size, size))

    def row_part(h, ch):
        return pl.ds(pl.multiple_of(h * piece + ch * size, size), size)

    def ag_copy(i, ch):
        to = (s, lax.rem(t + 1 + i, T))
        part = rows.at[row_part(t, ch)]
        return remote(part, part, ag_send.at[i, ch], ag_recv.at[i, ch], to)

    def unit(zs, i, ch, yy, cc):
        h = lax.rem(t + T - i, T)
        return pl.ds(pl.multiple_of((zs * 4 + yy * 2 + cc) * R + h * piece + ch * size, size), size)

    def uid(zs, i, ch):
        return (zs * T + i) * CHUNKS + ch

    def z_copy(zs, i, ch, sems, to):
        n = uid(zs, i, ch)
        part = cols.at[unit(zs, i, ch, y, c)]
        return remote(part, part, sems.at[n], z_recv.at[n], to)

    def y_copy(zs, i, ch, yy):
        n = uid(zs, i, ch)
        part = cols.at[unit(zs, i, ch, yy, c)]
        return remote(part, part, y_send.at[n], y_recv.at[n], y_mate)

    def c_copy(zs, i, ch, yy, cc, other):
        n = uid(zs, i, ch)
        part = cols.at[unit(zs, i, ch, yy, cc)]
        return remote(part, part, c_send.at[other, n], c_recv.at[other, n], c_mate)

    def goes_up(zs):
        return (own_z >= zs) & (z < Z - 1)

    def goes_down(zs):
        return (own_z <= zs) & (z > 0)

    def forward(zs, i, ch):
        @pl.when(goes_up(zs))
        def _():
            z_copy(zs, i, ch, up_send, z_up).start()

        @pl.when(goes_down(zs))
        def _():
            z_copy(zs, i, ch, down_send, z_down).start()

        y_copy(zs, i, ch, y).start()
        c_copy(zs, i, ch, y, c, 0).start()

    for ch in range(CHUNKS):
        part = pl.ds(ch * size, size)
        total = partial[T - 1, part, :]
        for i in range(T - 1):
            rs_copy(i, ch).wait_recv()
            total = total + landed[i, part, :]
        rounded = total.astype(jnp.bfloat16)
        rows[row_part(t, ch), :] = rounded
        for i in range(T - 1):
            ag_copy(i, ch).start()

        @pl.when(in_panel)
        def _():
            cols[unit(near, 0, ch, y, c), :] = rounded
            forward(near, 0, ch)

    order = [(j, i, ch) for j in range(ZP) for i in range(T) for ch in range(CHUNKS)]

    def pass_on(k):
        j, i, ch = order[k]
        zs = lax.rem(near + j, ZP)
        y_copy(zs, i, ch, 1 - y).wait_recv()
        c_copy(zs, i, ch, 1 - y, c, 1).start()

    for k, (j, i, ch) in enumerate(order):
        zs = lax.rem(near + j, ZP)

        def arrive(zs=zs, i=i, ch=ch):
            z_copy(zs, i, ch, up_send, z_up).wait_recv()
            forward(zs, i, ch)

        if j:
            arrive()
        else:
            pl.when(jnp.logical_not(in_panel))(arrive)
            if i:

                @pl.when(in_panel)
                def _():
                    ag_copy(i - 1, ch).wait_recv()
                    cols[unit(zs, i, ch, y, c), :] = rows[row_part(lax.rem(t + T - i, T), ch), :]
                    forward(zs, i, ch)

        if k >= LAG:
            pass_on(k - LAG)

    @pl.when(jnp.logical_not(in_panel))
    def _():
        for i in range(T - 1):
            for ch in range(CHUNKS):
                ag_copy(i, ch).wait_recv()

    for k in range(max(len(order) - LAG, 0), len(order)):
        pass_on(k)

    lane = lax.broadcasted_iota(jnp.int32, (1, WIDTH), 1)
    x = rows[...].astype(jnp.float32)
    square = x * x
    high = square.astype(jnp.bfloat16)
    low = (square - high.astype(jnp.float32)).astype(jnp.bfloat16)
    x = x * (1.0 / BINS)
    swapped = jnp.where(
        (lane // BINS) % 2 == 0, pltpu.roll(x, WIDTH - BINS, 1), -pltpu.roll(x, BINS, 1)
    )
    entry = lax.broadcasted_iota(jnp.int32, (WIDTH, 128), 0) // (2 * BINS)
    for b in range(BANDS):
        here = lane // (2 * BINS) == b
        lhs[2 * b] = jnp.where(here, x, 0.0).astype(jnp.bfloat16)
        lhs[2 * b + 1] = jnp.where(here, swapped, 0.0).astype(jnp.bfloat16)
        ones = jnp.where(entry == b, 1.0, 0.0).astype(jnp.bfloat16)
        power = jnp.dot(high, ones, preferred_element_type=jnp.float32)
        power = power + jnp.dot(low, ones, preferred_element_type=jnp.float32)
        rinv[b] = 1.0 / (power * (1.0 / BINS) + EPSILON)

    for j, i, ch in order:
        zs = lax.rem(near + j, ZP)
        c_copy(zs, i, ch, y, 1 - c, 0).wait_recv()
        c_copy(zs, i, ch, 1 - y, 1 - c, 1).wait_recv()

    for i in range(T - 1):
        for ch in range(CHUNKS):
            rs_copy(i, ch).wait_send()
            ag_copy(i, ch).wait_send()
    for j, i, ch in order:
        zs = lax.rem(near + j, ZP)

        @pl.when(goes_up(zs))
        def _():
            z_copy(zs, i, ch, up_send, z_up).wait_send()

        @pl.when(goes_down(zs))
        def _():
            z_copy(zs, i, ch, down_send, z_down).wait_send()

        y_copy(zs, i, ch, y).wait_send()
        c_copy(zs, i, ch, y, c, 0).wait_send()
        c_copy(zs, i, ch, 1 - y, c, 1).wait_send()


def gather_spectra(S, T, metrics, band_starts):
    R, L = metrics.shape
    owners = S // T
    piece = R // T
    units = owners // 4 * T * CHUNKS
    dma = pltpu.SemaphoreType.DMA
    vmem = pl.BlockSpec(memory_space=pltpu.VMEM)
    return pl.pallas_call(
        functools.partial(spectra_kernel, S, T),
        out_shape=(
            jax.ShapeDtypeStruct((owners * R, WIDTH), jnp.bfloat16),
            jax.ShapeDtypeStruct((2 * BANDS, R, WIDTH), jnp.bfloat16),
            jax.ShapeDtypeStruct((BANDS, R, 128), jnp.float32),
        ),
        in_specs=[pl.BlockSpec(memory_space=pltpu.SMEM), pl.BlockSpec(memory_space=pl.ANY)],
        out_specs=(vmem, vmem, vmem),
        scratch_shapes=[
            pltpu.VMEM((R, L), jnp.bfloat16),
            pltpu.VMEM((L, WIDTH), jnp.bfloat16),
            pltpu.VMEM((T, piece, WIDTH), jnp.float32),
            pltpu.VMEM((T - 1, piece, WIDTH), jnp.float32),
            pltpu.VMEM((R, WIDTH), jnp.bfloat16),
            dma,
            dma((T - 1, CHUNKS)),
            dma((T - 1, CHUNKS)),
            dma((T - 1, CHUNKS)),
            dma((T - 1, CHUNKS)),
            dma((units,)),
            dma((units,)),
            dma((units,)),
            dma((units,)),
            dma((units,)),
            dma((2, units)),
            dma((2, units)),
        ],
        compiler_params=pltpu.CompilerParams(
            collective_id=0, has_side_effects=True, vmem_limit_bytes=40 * 1024 * 1024
        ),
        name="spectra",
    )(band_starts, metrics)


def products_kernel(lhs, rinv, cols, cross, coherence, cinv):
    tile = cols.shape[0]

    @pl.when(pl.program_id(1) == 0)
    def _():
        x = cols[...].astype(jnp.float32)
        square = x * x
        high = square.astype(jnp.bfloat16)
        low = (square - high.astype(jnp.float32)).astype(jnp.bfloat16)
        band = lax.broadcasted_iota(jnp.int32, (16, WIDTH), 0)
        lane = lax.broadcasted_iota(jnp.int32, (16, WIDTH), 1)
        ones = jnp.where(lane // (2 * BINS) == band, 1.0, 0.0).astype(jnp.bfloat16)
        power = lax.dot_general(ones, high, NT, preferred_element_type=jnp.float32)
        power = power + lax.dot_general(ones, low, NT, preferred_element_type=jnp.float32)
        cinv[...] = 1.0 / (power * (1.0 / BINS) + EPSILON)

    right = cols[...]
    for b in range(BANDS):
        real = lax.dot_general(lhs[2 * b], right, NT, preferred_element_type=jnp.float32)
        imag = lax.dot_general(lhs[2 * b + 1], right, NT, preferred_element_type=jnp.float32)
        cross[b, 0] = real.astype(jnp.bfloat16)
        cross[b, 1] = imag.astype(jnp.bfloat16)
        row_scale = jnp.concatenate([rinv[b]] * (tile // 128), axis=1)
        coherence[b] = (real * real + imag * imag) * row_scale * cinv[b : b + 1, :]


def products(lhs, rinv, cols):
    R, C = lhs.shape[1], cols.shape[0]
    high, wide = 128, 512
    return pl.pallas_call(
        products_kernel,
        grid=(C // wide, R // high),
        out_shape=(
            jax.ShapeDtypeStruct((BANDS, 2, R, C), jnp.bfloat16),
            jax.ShapeDtypeStruct((BANDS, R, C), jnp.float32),
        ),
        in_specs=[
            pl.BlockSpec((2 * BANDS, high, WIDTH), lambda j, i: (0, i, 0)),
            pl.BlockSpec((BANDS, high, 128), lambda j, i: (0, i, 0)),
            pl.BlockSpec((wide, WIDTH), lambda j, i: (j, 0)),
        ],
        out_specs=(
            pl.BlockSpec((BANDS, 2, high, wide), lambda j, i: (0, 0, i, j)),
            pl.BlockSpec((BANDS, high, wide), lambda j, i: (0, i, j)),
        ),
        scratch_shapes=[pltpu.VMEM((16, wide), jnp.float32)],
        compiler_params=pltpu.CompilerParams(vmem_limit_bytes=40 * 1024 * 1024),
        name="products",
    )(lhs, rinv, cols)


def solution(mesh):
    S, T = mesh.shape["svc"], mesh.shape["tm"]

    def body(metrics, band_starts):
        cols, lhs, rinv = gather_spectra(S, T, metrics, band_starts)
        return products(lhs, rinv, cols)

    return jax.shard_map(
        body,
        mesh=mesh,
        in_specs=(P("svc", "tm"), P()),
        out_specs=(P(None, None, "svc", "tm"), P(None, "svc", "tm")),
        check_vma=False,
    )
```
